256 devices in a mesh: band: 8 (over z_hi, y), row: 32 (over z_lo, x, core).
Axes of the slice: x: 4, y: 4, z: 8 (z_hi: 2, z_lo: 4; z = z_hi * 4 + z_lo), core: 2. Of those that a mesh axis runs over, the one named last changes fastest.
Arguments:
- gebhart: bfloat16 [8, 2048, 65536], P('band', None, 'row'), may hold values from -0.046875 to 0.046875
- temps: float32 [256, 65536], P(None, 'row'), may hold values from 150 to 400
- emissivity: float32 [8, 65536], P('band', 'row'), may hold values from 0.1 to 0.95
- band_edges: int32 [8, 2], P('band'), may hold values from 3000 to 26998, as said below
- conductance: float32 [2048], P('row'), may hold values from 0.0005 to 0.005
- neighbours: int32 [2048, 4], P('row'), may hold values from 0 to 2047, as said below
Outputs:
- absorbed: float32 [256, 2048], P(None, 'row')
- heating: float32 [256, 2048], P(None, 'row')
The draws below stay inside these ranges and needn't reach their ends.
Inputs may be any that keep to these rules, and one draw needn't show every extreme that they name: `band_edges`: each band's lower edge lies below its upper edge; bands rise with the band index. `neighbours`: every neighbour lies at most 64 window indices away from its panel, counted cyclically over 2048; that distance is reached.
All inputs are finite; a program needn't handle non-finite values.
Results may differ from the reference program's by a relative error of at most 0.0029.
Values sent between devices are 32-bit elements; how exact they have to be, the bound alone decides.
No kernel may reach another device: no remote copies, remote signals or barrier semaphores. Data moves between devices by JAX's collectives and lax.ppermute only.
A program may use at most 64 MiB of HBM per device.

```python
import math
import jax
import jax.numpy as jnp
from jax import lax

P_SIZE = 65536
BANDS = 8
K = 256
ROWS_DEV = 64
PB = 2048
W = 2048
N_ROW = 32


def draw_band_edges(key, part):
    key = jax.random.fold_in(key, 11)
    first, second = jax.random.split(key)
    index = jnp.arange(BANDS, dtype=jnp.int32)
    lower = 3000 + 3000 * index + jax.random.randint(first, (BANDS,), 0, 1500, dtype=jnp.int32)
    lower = lower.at[0].set(3000)
    upper = lower + 1000 + jax.random.randint(second, (BANDS,), 0, 1500, dtype=jnp.int32)
    upper = upper.at[BANDS - 1].set(3000 * BANDS + 2998)
    return jnp.stack([lower, upper], axis=1).astype(jnp.int32)


def draw_neighbours(key, part):
    key = jax.random.fold_in(key, 23)
    offsets = jax.random.randint(key, (W, 4), -ROWS_DEV, ROWS_DEV + 1, dtype=jnp.int32)
    offsets = offsets.at[0, 0].set(ROWS_DEV).at[1, 1].set(-ROWS_DEV)
    panels = jnp.arange(W, dtype=jnp.int32)
    return jnp.mod(panels[:, None] + offsets, W).astype(jnp.int32)


def raised(entries, stream_key, source, target, parts, factor):
    owner, partner = [(jnp.arange(entries.shape[position]) // (entries.shape[position] // parts)).reshape([-1 if axis == position else 1 for axis in range(entries.ndim)]) for position in (source, target)]
    chosen = jax.random.permutation(stream_key, parts)[partner]
    strong = (owner == chosen) | (owner == (partner + parts // 2) % parts)
    return jnp.where(strong, factor * entries, entries)


def block_scale(own_key, dims, cuts, smallest, high):
    factor_of, own = 1.0, jax.random.fold_in(own_key, 6)
    for axis_at, blocks in cuts:
        heights = jnp.exp(jax.random.uniform(jax.random.fold_in(own, axis_at), (blocks,), jnp.float32, smallest / len(cuts), high / len(cuts)))
        factor_of = factor_of * jnp.repeat(heights, dims[axis_at] // blocks).reshape([-1 if axis == axis_at else 1 for axis in range(len(dims))])
    return factor_of


def heavy_noise(key, dims, width, reach, shards, heavy, kind=jnp.bfloat16):
    drawn = width * jax.random.normal(key, dims, jnp.float32)
    if shards:
        drawn = drawn * block_scale(key, dims, shards, -0.22, 0.18)
    return jnp.clip(raised(drawn, jax.random.fold_in(key, 3), *heavy), -reach, reach).astype(kind)


def setup_inputs(seed: int = 0) -> dict:
    keys = jax.random.split(jax.random.key(seed), 7)
    gebhart = heavy_noise(keys[0], (BANDS, W, P_SIZE), P_SIZE ** -0.5, 0.046875, ((0, 8), (2, 32)), (2, 1, 32, 2.75))
    temps = jnp.clip(150.0 + 250.0 * jax.random.uniform(keys[1], (K, P_SIZE), jnp.float32) ** block_scale(keys[1], (K, P_SIZE), ((1, 32),), -0.2, 0.2), 150.0, 400.0)
    emissivity = jnp.clip(0.1 + 0.84999999 * jax.random.uniform(keys[2], (BANDS, P_SIZE), jnp.float32) ** block_scale(keys[2], (BANDS, P_SIZE), ((0, 8), (1, 32)), -0.2, 0.2), 0.1, 0.95)
    band_edges = draw_band_edges(jax.random.fold_in(keys[6], 71), 0)
    conductance = jnp.clip(jnp.exp(math.log(0.005) - 2.30258502 * jax.random.uniform(keys[4], (W,), jnp.float32) ** block_scale(keys[4], (W,), ((0, 32),), -0.2, 0.2)), 0.0005, 0.005)
    neighbours = draw_neighbours(jax.random.fold_in(keys[6], 71), 0)
    return dict(gebhart=gebhart, temps=temps, emissivity=emissivity, band_edges=band_edges, conductance=conductance, neighbours=neighbours)


def cumulative(edge, temps):
    z = 14388000.0 / (edge * temps)
    return (15.0 / math.pi ** 4) * jnp.exp(-z) * (((z + 3.0) * z + 6.0) * z + 6.0)


def band_power(temps, emissivity, band_edges):
    lower = band_edges[:, 0].astype(jnp.float32)[:, None, None]
    upper = band_edges[:, 1].astype(jnp.float32)[:, None, None]
    heat = temps[None, :, :]
    fraction = cumulative(upper, heat) - cumulative(lower, heat)
    scale = (heat / 300.0) ** 4
    return (emissivity[:, None, :] * fraction * scale).astype(jnp.bfloat16)


def reference(gebhart, temps, emissivity, band_edges, conductance, neighbours):
    power = band_power(temps, emissivity, band_edges)

    def one_band(total, pair):
        factors, emitted = pair
        return total + jnp.dot(factors, emitted.T, preferred_element_type=jnp.float32), None

    start = jnp.zeros((W, K), jnp.float32)
    total, unused = lax.scan(one_band, start, (gebhart, power))
    absorbed = total.T
    own = power.reshape(BANDS, K, N_ROW, PB)[:, :, :, :ROWS_DEV].reshape(BANDS, K, W)
    emitted = jnp.sum(own.astype(jnp.float32), axis=0)
    window = temps.reshape(K, N_ROW, PB)[:, :, :ROWS_DEV].reshape(K, W)
    nearby = window[:, neighbours]
    heating = absorbed - emitted + conductance[None, :] * jnp.sum(nearby - window[:, :, None], axis=2)
    return absorbed, heating
```

```python
import math

import jax
import jax.numpy as jnp
from jax import lax
from jax.experimental import pallas as pl
from jax.experimental.pallas import tpu as pltpu
from jax.sharding import PartitionSpec as P

ROWS = 64
NX, NZ, NY = 4, 4, 4
F32 = jnp.float32
VMEM = pltpu.VMEM
LOG2E = 1.0 / math.log(2.0)
PARAMS = dict(vmem_limit_bytes=48 * 2**20)


def vspec(count):
    return [pl.BlockSpec(memory_space=VMEM)] * count


def sds(*shape, dtype=F32):
    return jax.ShapeDtypeStruct(shape, dtype)


def place():
    row = lax.axis_index("row")
    return row // (2 * NX), (row // 2) % NX, row % 2


def power_chunk(t, emis, a_lo, a_hi):
    r = pl.reciprocal(t, approx=True)
    r = r * (2.0 - t * r)
    lo = a_lo * r
    hi = a_hi * r
    cum_lo = jnp.exp2(lo * -LOG2E) * (((lo + 3.0) * lo + 6.0) * lo + 6.0)
    cum_hi = jnp.exp2(hi * -LOG2E) * (((hi + 3.0) * hi + 6.0) * hi + 6.0)
    square = t * t
    return (cum_hi - cum_lo) * (square * square) * emis


def dot_nt(a, b):
    return lax.dot_general(a, b, (((1,), (1,)), ((), ())), preferred_element_type=F32)


def gather_rows(g_hbm, gbuf, sems, x, core):
    return [
        pltpu.make_async_copy(g_hbm.at[:, (x + d) % NX, core], gbuf.at[d], sems.at[d])
        for d in range(NX)
    ]


def first_kernel(edges, emis, t_hbm, g_hbm, u, p, em, win, tbuf, gbuf, scaled, tsem, gsem):
    z, x, core = place()
    orbits = tbuf.shape[0]
    part = orbits // 4
    tcopies = [
        pltpu.make_async_copy(
            t_hbm.at[pl.ds(i * part, part)], tbuf.at[pl.ds(i * part, part)], tsem.at[i]
        )
        for i in range(4)
    ]
    for c in tcopies:
        c.start()
    gcopies = gather_rows(g_hbm, gbuf, gsem, x, 1 - core)
    for c in gcopies:
        c.start()
    a_lo = 14388000.0 / jnp.full((1, 512), edges[0, 0].astype(F32))
    a_hi = 14388000.0 / jnp.full((1, 512), edges[0, 1].astype(F32))
    scaled[...] = emis[...] * (15.0 / math.pi**4 / 300.0**4)
    for i in range(4):
        tcopies[i].wait()

        @pl.loop(0, part // 16)
        def _(j):
            rows = pl.ds(i * part + j * 16, 16)
            for c in range(4):
                cols = pl.ds(c * 512, 512)
                p[rows, cols] = power_chunk(
                    tbuf[rows, cols], scaled[:, cols], a_lo, a_hi
                ).astype(jnp.bfloat16)

    win[...] = tbuf[:, :128].T[:ROWS]
    em[...] = p[:, :128].astype(F32).T[:ROWS]
    for d in range(NX):
        gcopies[d].wait()
        g = gbuf[d].reshape(NZ * ROWS, gbuf.shape[3])
        u[d] = dot_nt(g, p[...])


def second_kernel(p, g_hbm, t, gbuf, gsem):
    z, x, core = place()
    gcopies = gather_rows(g_hbm, gbuf, gsem, x, core)
    for c in gcopies:
        c.start()
    for d in range(NX):
        gcopies[d].wait()
        g = gbuf[d].reshape(NZ * ROWS, gbuf.shape[3])
        t[d] = dot_nt(g, p[...])


def add_kernel(t, u, *outs):
    for d in range(NX):
        outs[d][...] = t[d] + u[d]


def x_sum_kernel(a, b, c, d, *outs):
    z, x, core = place()
    for i in range(NZ):
        rows = pl.ds(pl.multiple_of(((z + i) % NZ) * ROWS, ROWS), ROWS)
        outs[i][...] = (a[rows] + b[rows]) + (c[rows] + d[rows])


def sum_kernel(a, b, c, d, out):
    out[...] = (a[...] + b[...]) + (c[...] + d[...])


def pair_kernel(a, b, c, d, e, out):
    out[:ROWS] = (a[...] + b[...]) + (c[...] + d[...])
    out[ROWS:] = e[...]


def conduct_kernel(neighbours, low, window, high, out):
    z, x, core = place()
    mine = (z * NX + x) * 2 + core
    total = 32 * ROWS
    local = neighbours[...] - (mine * ROWS - ROWS)
    local = jnp.where(local < 0, local + total, local)
    local = jnp.where(local >= total, local - total, local)
    column = lax.broadcasted_iota(jnp.int32, (ROWS, ROWS), 1)
    acc = -4.0 * window[...]
    for i, block in enumerate((low, window, high)):
        count = jnp.zeros((ROWS, ROWS), F32)
        for j in range(4):
            count += jnp.where(local[:, j : j + 1] == column + i * ROWS, 1.0, 0.0)
        acc += jnp.dot(
            count, block[...], precision=lax.Precision.HIGHEST, preferred_element_type=F32
        )
    out[...] = acc


def last_kernel(mine, other, lap, conductance, absorbed, heating):
    a = mine[:ROWS] + other[:ROWS]
    e = mine[ROWS:] + other[ROWS:]
    at = a.T
    absorbed[...] = at
    heating[...] = at - e.T + conductance[...] * lap[...].T


def call(kernel, count, out_shape, scratch=(), in_specs=None, cost=None):
    single = not isinstance(out_shape, (list, tuple))
    return pl.pallas_call(
        kernel,
        out_shape=out_shape,
        in_specs=in_specs if in_specs is not None else vspec(count),
        out_specs=vspec(1)[0] if single else vspec(len(out_shape)),
        scratch_shapes=list(scratch),
        compiler_params=pltpu.CompilerParams(**PARAMS),
        cost_estimate=cost,
    )


def row_perm(move):
    return [
        ((z * NX + x) * 2 + c, (lambda a: (a[0] * NX + a[1]) * 2 + a[2])(move(z, x, c)))
        for z in range(NZ)
        for x in range(NX)
        for c in range(2)
    ]


CORE = row_perm(lambda z, x, c: (z, x, 1 - c))
XS = [row_perm(lambda z, x, c, d=d: (z, (x + d) % NX, c)) for d in range(NX)]
ZS = [row_perm(lambda z, x, c, d=d: ((z + d) % NZ, x, c)) for d in range(NZ)]
UP = [(i, (i + 1) % 32) for i in range(32)]
DOWN = [(i, (i - 1) % 32) for i in range(32)]
YS = [[(h * NY + y, h * NY + (y + d) % NY) for h in range(2) for y in range(NY)] for d in range(NY)]
HI = [(i, (i + NY) % (2 * NY)) for i in range(2 * NY)]


def body(gebhart, temps, emissivity, band_edges, conductance, neighbours):
    orbits, panels = temps.shape
    g = gebhart.reshape(NZ, NX, 2, ROWS, panels)
    half = NZ * ROWS
    hbm = pl.BlockSpec(memory_space=pl.ANY)
    gb = [VMEM((NX, NZ, ROWS, panels), jnp.bfloat16)]
    cost = pl.CostEstimate(
        flops=2 * NX * half * panels * orbits, bytes_accessed=8 * 2**20, transcendentals=0
    )
    u, p, em, win = call(
        first_kernel,
        4,
        [
            sds(NX, half, orbits),
            sds(orbits, panels, dtype=jnp.bfloat16),
            sds(ROWS, orbits),
            sds(ROWS, orbits),
        ],
        in_specs=[pl.BlockSpec(memory_space=pltpu.SMEM), vspec(1)[0], hbm, hbm],
        scratch=[
            VMEM((orbits, panels), F32),
            *gb,
            VMEM((1, panels), F32),
            pltpu.SemaphoreType.DMA((4,)),
            pltpu.SemaphoreType.DMA((NX,)),
        ],
        cost=cost,
    )(band_edges, emissivity, temps, g)
    u_in = lax.ppermute(u, "row", CORE)
    t = call(
        second_kernel,
        2,
        sds(NX, half, orbits),
        in_specs=[vspec(1)[0], hbm],
        scratch=[*gb, pltpu.SemaphoreType.DMA((NX,))],
        cost=cost,
    )(p, g)
    s = call(add_kernel, 2, [sds(half, orbits)] * NX)(t, u_in)
    x2 = lax.ppermute(s[2], "row", XS[2])
    x1 = lax.ppermute(s[1], "row", XS[1])
    x3 = lax.ppermute(s[3], "row", XS[3])
    low = lax.ppermute(win, "row", UP)
    high = lax.ppermute(win, "row", DOWN)
    e_in = [lax.ppermute(em, "band", YS[d]) for d in (1, 2, 3)]
    e = call(sum_kernel, 4, sds(ROWS, orbits))(em, *e_in)
    lap = call(conduct_kernel, 4, sds(ROWS, orbits))(neighbours, low, win, high)
    zs = call(x_sum_kernel, 4, [sds(ROWS, orbits)] * NZ)(s[0], x1, x2, x3)
    z_in = [lax.ppermute(zs[d], "row", ZS[d]) for d in (1, 2, 3)]
    ysum = call(sum_kernel, 4, sds(ROWS, orbits))(zs[0], *z_in)
    y_in = [lax.ppermute(ysum, "band", YS[d]) for d in (1, 2, 3)]
    pair = call(pair_kernel, 5, sds(2 * ROWS, orbits))(ysum, *y_in, e)
    other = lax.ppermute(pair, "band", HI)
    absorbed, heating = call(last_kernel, 4, [sds(orbits, ROWS)] * 2)(
        pair, other, lap, conductance.reshape(1, ROWS)
    )
    return absorbed, heating


def solution(mesh):
    return jax.shard_map(
        body,
        mesh=mesh,
        in_specs=(
            P("band", None, "row"),
            P(None, "row"),
            P("band", "row"),
            P("band", None),
            P("row"),
            P("row", None),
        ),
        out_specs=(P(None, "row"), P(None, "row")),
        check_vma=False,
    )
```

```python
import math

import jax
import jax.numpy as jnp
from jax import lax
from jax.experimental import pallas as pl
from jax.experimental.pallas import tpu as pltpu
from jax.sharding import PartitionSpec as P

ROWS = 64
NX, NZ, NY = 4, 4, 4
F32 = jnp.float32
VMEM = pltpu.VMEM
LOG2E = 1.0 / math.log(2.0)
PARAMS = dict(vmem_limit_bytes=24 * 2**20)


def vspec(count):
    return [pl.BlockSpec(memory_space=VMEM)] * count


def sds(*shape, dtype=F32):
    return jax.ShapeDtypeStruct(shape, dtype)


def place():
    row = lax.axis_index("row")
    return row // (2 * NX), (row // 2) % NX, row % 2


def power_chunk(t, emis, a_lo, a_hi):
    r = pl.reciprocal(t, approx=True)
    r = r * (2.0 - t * r)
    lo = a_lo * r
    hi = a_hi * r
    cum_lo = jnp.exp2(lo * -LOG2E) * (((lo + 3.0) * lo + 6.0) * lo + 6.0)
    cum_hi = jnp.exp2(hi * -LOG2E) * (((hi + 3.0) * hi + 6.0) * hi + 6.0)
    square = t * t
    return (cum_hi - cum_lo) * (square * square) * emis


def dot_nt(a, b):
    return lax.dot_general(a, b, (((1,), (1,)), ((), ())), preferred_element_type=F32)


def gather_rows(g_hbm, gbuf, sems, x, core):
    return [
        pltpu.make_async_copy(g_hbm.at[:, (x + d) % NX, core], gbuf.at[d], sems.at[d])
        for d in range(NX)
    ]


def first_kernel(
    edges_hbm, emis_hbm, t_hbm, g_hbm, u, p, gown, win, par, tbuf, gbuf, scaled, edges, tsem, gsem, osem, ssem
):
    z, x, core = place()
    part = tbuf.shape[0] // 4
    small = [
        pltpu.make_async_copy(edges_hbm, edges, ssem.at[0]),
        pltpu.make_async_copy(emis_hbm, scaled, ssem.at[1]),
    ]
    tcopies = [
        pltpu.make_async_copy(
            t_hbm.at[pl.ds(i * part, part)], tbuf.at[pl.ds(i * part, part)], tsem.at[i]
        )
        for i in range(4)
    ]
    gcopies = gather_rows(g_hbm, gbuf, gsem, x, 1 - core)
    ocopies = gather_rows(g_hbm, gown, osem, x, core)
    for c in small + tcopies + gcopies + ocopies:
        c.start()
    for c in small:
        c.wait()
    a_lo = 14388000.0 / jnp.full((1, 512), edges[0, 0].astype(F32))
    a_hi = 14388000.0 / jnp.full((1, 512), edges[0, 1].astype(F32))
    scaled[...] = scaled[...] * (15.0 / math.pi**4 / 300.0**4)
    lane = lax.broadcasted_iota(jnp.int32, (8, 256), 1)
    line = jnp.broadcast_to(scaled[:, :256], (8, 256))
    line = jnp.where(lane == ROWS, a_lo[:, :256], line)
    par[...] = jnp.where(lane == ROWS + 1, a_hi[:, :256], line)
    for i in range(4):
        tcopies[i].wait()

        @pl.loop(0, part // 16)
        def _(j):
            rows = pl.ds(i * part + j * 16, 16)
            for c in range(4):
                cols = pl.ds(c * 512, 512)
                p[rows, cols] = power_chunk(
                    tbuf[rows, cols], scaled[:, cols], a_lo, a_hi
                ).astype(jnp.bfloat16)

    half = NZ * ROWS
    w = tbuf[:, :128].T[:ROWS]
    win[...] = w
    u[NX * half :] = w
    for d in range(NX):
        gcopies[d].wait()
        u[d * half : (d + 1) * half] = dot_nt(gbuf[d].reshape(half, gbuf.shape[3]), p[...])
    for c in ocopies:
        c.wait()


def second_kernel(p, g, t):
    for d in range(NX):
        t[d] = dot_nt(g[d].reshape(NZ * ROWS, g.shape[3]), p[...])


def add_kernel(t, u, *outs):
    half = NZ * ROWS
    for d in range(NX):
        outs[d][...] = t[d] + u[d * half : (d + 1) * half]
    outs[NX][...] = u[NX * half :]


def x_sum_kernel(a, b, c, d, *outs):
    z, x, core = place()
    for i in range(NZ):
        rows = pl.ds(pl.multiple_of(((z + i) % NZ) * ROWS, ROWS), ROWS)
        outs[i][...] = (a[rows] + b[rows]) + (c[rows] + d[rows])


def z_sum_kernel(a, b, c, d, par, cross, out):
    out[:ROWS] = (a[...] + b[...]) + (c[...] + d[...])
    out[ROWS:] = par[...]


def y_sum_kernel(a, b, c, d, out):
    out[:ROWS] = (a[:ROWS] + b[:ROWS]) + (c[:ROWS] + d[:ROWS])
    for i, ref in enumerate((a, b, c, d)):
        out[ROWS + i : ROWS + i + 1] = ref[ROWS : ROWS + 1]
    out[ROWS + NY :] = jnp.zeros((8 - NY, out.shape[1]), F32)


def emitted(par, win):
    total = jnp.zeros(win.shape, F32)
    columns = jnp.broadcast_to(par, (8, par.shape[1]))[:, :128].T
    for i in range(NY):
        part = power_chunk(
            win, columns[:ROWS, i : i + 1], par[i, ROWS], par[i, ROWS + 1]
        )
        total += part.astype(jnp.bfloat16).astype(F32)
    return total


def side_kernel(neighbours, conductance, swapped, window, cross, mine, out):
    z, x, core = place()
    me = (z * NX + x) * 2 + core
    total = 32 * ROWS
    local = neighbours[...] - (me * ROWS - ROWS)
    local = jnp.where(local < 0, local + total, local)
    local = jnp.where(local >= total, local - total, local)
    row = lax.broadcasted_iota(jnp.int32, (ROWS, ROWS), 0)
    lane = lax.broadcasted_iota(jnp.int32, (ROWS, ROWS), 1)
    low = jnp.where(core == 0, cross[...], swapped[...])
    high = jnp.where(core == 0, swapped[...], cross[...])
    acc = -emitted(mine[ROWS:], window[...])
    for i, block in enumerate((low, window[...], high)):
        count = jnp.where(row == lane, -4.0, 0.0) if i == 1 else jnp.zeros((ROWS, ROWS), F32)
        for j in range(4):
            count += jnp.where(local[j : j + 1] == row + i * ROWS, 1.0, 0.0)
        acc += lax.dot_general(
            count * conductance[...],
            block,
            (((0,), (0,)), ((), ())),
            precision=lax.Precision.HIGHEST,
            preferred_element_type=F32,
        )
    out[...] = acc


def last_kernel(mine, other, side, window, absorbed, heating):
    a = mine[:ROWS] + other[:ROWS]
    absorbed[...] = a
    heating[...] = a + side[...] - emitted(other[ROWS:], window[...])


def call(kernel, count, out_shape, scratch=(), in_specs=None, cost=None):
    single = not isinstance(out_shape, (list, tuple))
    return pl.pallas_call(
        kernel,
        out_shape=out_shape,
        in_specs=in_specs if in_specs is not None else vspec(count),
        out_specs=vspec(1)[0] if single else vspec(len(out_shape)),
        scratch_shapes=list(scratch),
        compiler_params=pltpu.CompilerParams(**PARAMS),
        cost_estimate=cost,
    )


def row_perm(move):
    return [
        ((z * NX + x) * 2 + c, (lambda a: (a[0] * NX + a[1]) * 2 + a[2])(move(z, x, c)))
        for z in range(NZ)
        for x in range(NX)
        for c in range(2)
    ]


CORE = row_perm(lambda z, x, c: (z, x, 1 - c))
XS = [row_perm(lambda z, x, c, d=d: (z, (x + d) % NX, c)) for d in range(NX)]
ZS = [row_perm(lambda z, x, c, d=d: ((z + d) % NZ, x, c)) for d in range(NZ)]
CROSS = [(i, (i + 1 if i % 2 else i - 1) % 32) for i in range(32)]
YS = [[(h * NY + y, h * NY + (y + d) % NY) for h in range(2) for y in range(NY)] for d in range(NY)]
HI = [(i, (i + NY) % (2 * NY)) for i in range(2 * NY)]


def body(gebhart, temps, emissivity, band_edges, conductance, neighbours):
    orbits, panels = temps.shape
    g = gebhart.reshape(NZ, NX, 2, ROWS, panels)
    half = NZ * ROWS
    hbm = pl.BlockSpec(memory_space=pltpu.HBM)
    bf = jnp.bfloat16
    dma = pltpu.SemaphoreType.DMA
    block = sds(ROWS, orbits)
    message = sds(ROWS + 8, orbits)
    cost = pl.CostEstimate(
        flops=2 * NX * half * panels * orbits, bytes_accessed=8 * 2**20, transcendentals=0
    )
    far = [
        pltpu.with_memory_space_constraint(a, pltpu.HBM)
        for a in (band_edges, emissivity, temps, g)
    ]
    u, p, gown, win, par = call(
        first_kernel,
        4,
        [
            sds(NX * half + ROWS, orbits),
            sds(orbits, panels, dtype=bf),
            sds(NX, NZ, ROWS, panels, dtype=bf),
            block,
            sds(8, orbits),
        ],
        in_specs=[hbm] * 4,
        scratch=[
            VMEM((orbits, panels), F32),
            VMEM((NX, NZ, ROWS, panels), bf),
            VMEM((1, panels), F32),
            pltpu.SMEM((1, 2), jnp.int32),
            dma((4,)),
            dma((NX,)),
            dma((NX,)),
            dma((2,)),
        ],
        cost=cost,
    )(*far)
    u_in = lax.ppermute(u, "row", CORE)
    t = call(second_kernel, 2, sds(NX, half, orbits), cost=cost)(p, gown)
    *s, swapped = call(add_kernel, 2, [sds(half, orbits)] * NX + [block])(t, u_in)
    x2 = lax.ppermute(s[2], "row", XS[2])
    x1 = lax.ppermute(s[1], "row", XS[1])
    x3 = lax.ppermute(s[3], "row", XS[3])
    cross = lax.ppermute(win, "row", CROSS)
    zs = call(x_sum_kernel, 4, [block] * NZ)(s[0], x1, x2, x3)
    z_in = [lax.ppermute(zs[d], "row", ZS[d]) for d in (1, 2, 3)]
    zsum = call(z_sum_kernel, 6, message)(zs[0], *z_in, par, cross)
    y_in = [lax.ppermute(zsum, "band", YS[d]) for d in (1, 2, 3)]
    mine = call(y_sum_kernel, 4, message)(zsum, *y_in)
    other = lax.ppermute(mine, "band", HI)
    side = call(side_kernel, 6, block)(
        neighbours.T, conductance.reshape(1, ROWS), swapped, win, cross, mine
    )
    absorbed, heating = call(last_kernel, 4, [block] * 2)(mine, other, side, win)
    return absorbed.T, heating.T


def solution(mesh):
    return jax.shard_map(
        body,
        mesh=mesh,
        in_specs=(
            P("band", None, "row"),
            P(None, "row"),
            P("band", "row"),
            P("band", None),
            P("row"),
            P("row", None),
        ),
        out_specs=(P(None, "row"), P(None, "row")),
        check_vma=False,
    )
```

```python
import math

import jax
import jax.numpy as jnp
from jax import lax
from jax.experimental import pallas as pl
from jax.experimental.pallas import tpu as pltpu
from jax.sharding import PartitionSpec as P

ROWS = 64
NX, NZ, NY = 4, 4, 4
F32 = jnp.float32
VMEM = pltpu.VMEM
PART = 2 * NX * ROWS
FIRST, SECOND = (2, 1), (3, 0)
PRODUCT_FLOPS = 2 * PART * 2048 * 16
PAUSE_FLOPS = 4 * 10**9
POWER_SCALE = 6.0 * 15.0 / math.pi**4 / 300.0**4
LOG2E = 1.0 / math.log(2.0)
PARAMS = dict(vmem_limit_bytes=24 * 2**20)


def vspec(count):
    return [pl.BlockSpec(memory_space=VMEM)] * count


def sds(*shape, dtype=F32):
    return jax.ShapeDtypeStruct(shape, dtype)


def place():
    row = lax.axis_index("row")
    return row // (2 * NX), (row // 2) % NX, row % 2


def edge_terms(a):
    return a * -LOG2E, a, a * a * 0.5, a * a * a * (1.0 / 6.0)


def power_chunk(t, emis, lo, hi):
    r = pl.reciprocal(t, approx=True)
    r = r * (2.0 - t * r)
    parts = [
        jnp.exp2(scale * r) * (((a + t) * t + half_square) * t + sixth_cube)
        for scale, a, half_square, sixth_cube in (lo, hi)
    ]
    return (parts[1] - parts[0]) * (t * emis)


def dot_nt(a, b):
    return lax.dot_general(a, b, (((1,), (1,)), ((), ())), preferred_element_type=F32)


def fetch_rows(g_hbm, buf, sems, z, core, offsets):
    return [
        pltpu.make_async_copy(g_hbm.at[(z + d) % NZ, :, core], buf.at[i], sems.at[i])
        for i, d in enumerate(offsets)
    ]


def flat(g):
    return g[...].reshape(g.shape[0] * NX * ROWS, g.shape[3])


def first_kernel(
    edges_hbm, emis_hbm, t_hbm, g_hbm, u, p, g1, g2, g3, win, par, tbuf, gbuf, scaled, edges, tsem, gsem, ssem
):
    z, x, core = place()
    part = tbuf.shape[0] // 4
    small = [
        pltpu.make_async_copy(edges_hbm, edges, ssem.at[0]),
        pltpu.make_async_copy(emis_hbm, scaled, ssem.at[1]),
    ]
    tcopies = [
        pltpu.make_async_copy(
            t_hbm.at[pl.ds(i * part, part)], tbuf.at[pl.ds(i * part, part)], tsem.at[i]
        )
        for i in range(4)
    ]
    gcopies = [
        fetch_rows(g_hbm, gbuf, gsem.at[0], z, 1 - core, FIRST),
        fetch_rows(g_hbm, g1, gsem.at[1], z, 1 - core, SECOND),
        fetch_rows(g_hbm, g2, gsem.at[2], z, core, FIRST),
        fetch_rows(g_hbm, g3, gsem.at[3], z, core, SECOND),
    ]
    for c in small + tcopies:
        c.start()
    for c in small:
        c.wait()
    a_lo = 14388000.0 / jnp.full((1, 512), edges[0, 0].astype(F32))
    a_hi = 14388000.0 / jnp.full((1, 512), edges[0, 1].astype(F32))
    scaled[...] = scaled[...] * POWER_SCALE
    lane = lax.broadcasted_iota(jnp.int32, (8, 256), 1)
    line = jnp.broadcast_to(scaled[:, :256], (8, 256))
    line = jnp.where(lane == ROWS, a_lo[:, :256], line)
    par[...] = jnp.where(lane == ROWS + 1, a_hi[:, :256], line)
    lo, hi = edge_terms(a_lo), edge_terms(a_hi)
    for i in range(4):
        tcopies[i].wait()
        if i == 1:
            for c in gcopies[0] + gcopies[1] + gcopies[2] + gcopies[3]:
                c.start()

        @pl.loop(0, part // 16)
        def _(j):
            rows = pl.ds(i * part + j * 16, 16)
            for c in range(4):
                cols = pl.ds(c * 512, 512)
                p[rows, cols] = power_chunk(tbuf[rows, cols], scaled[:, cols], lo, hi).astype(
                    jnp.bfloat16
                )

    w = tbuf[:, :128].T[:ROWS]
    win[...] = w
    u[PART:] = w
    for c in gcopies[0]:
        c.wait()
    u[:PART] = dot_nt(flat(gbuf), p[...])
    for c in gcopies[1] + gcopies[2] + gcopies[3]:
        c.wait()


def product_kernel(p, g, *refs):
    t = refs[-1]
    t[...] = dot_nt(flat(g), p[...])


def spread(value, outs):
    z, x, core = place()
    for d in range(NX):
        for i in range(2):
            rows = pl.ds(pl.multiple_of((i * NX + (x + d) % NX) * ROWS, ROWS), ROWS)
            outs[d][i * ROWS : (i + 1) * ROWS] = value(rows)


def add_kernel(t, u, *outs):
    spread(lambda rows: t[rows] + u[rows], outs)
    outs[NX][...] = u[PART:]


def product_add_kernel(p, g, u, s, *refs):
    outs, t = refs[:-1], refs[-1]
    t[...] = dot_nt(flat(g), p[...])
    spread(lambda rows: t[rows] + u[rows], outs)


def x_sum_carry_kernel(a, b, c, d, win, *outs):
    x_sum_kernel(a, b, c, d, *outs)
    outs[2][...] = win[...]


def x_sum_kernel(a, b, c, d, *outs):
    for i in range(2):
        rows = pl.ds(i * ROWS, ROWS)
        outs[i][...] = (a[rows] + b[rows]) + (c[rows] + d[rows])


def z_sum_kernel(a, b, c, d, par, cross, out):
    out[:ROWS] = (a[...] + b[...]) + (c[...] + d[...])
    out[ROWS:] = par[...]


def y_sum_kernel(a, b, c, d, out):
    out[:ROWS] = (a[:ROWS] + b[:ROWS]) + (c[:ROWS] + d[:ROWS])
    for i, ref in enumerate((a, b, c, d)):
        out[ROWS + i : ROWS + i + 1] = ref[ROWS : ROWS + 1]
    out[ROWS + NY :] = jnp.zeros((8 - NY, out.shape[1]), F32)


def emitted(par, win):
    total = jnp.zeros(win.shape, F32)
    columns = jnp.broadcast_to(par, (8, par.shape[1]))[:, :128].T
    for i in range(NY):
        part = power_chunk(
            win,
            columns[:ROWS, i : i + 1],
            edge_terms(par[i, ROWS]),
            edge_terms(par[i, ROWS + 1]),
        )
        total += part.astype(jnp.bfloat16).astype(F32)
    return total


def side_kernel(neighbours, conductance, swapped, window, cross, mine, out):
    z, x, core = place()
    me = (z * NX + x) * 2 + core
    total = 32 * ROWS
    local = neighbours[...] - (me * ROWS - ROWS)
    local = jnp.where(local < 0, local + total, local)
    local = jnp.where(local >= total, local - total, local)
    row = lax.broadcasted_iota(jnp.int32, (ROWS, ROWS), 0)
    lane = lax.broadcasted_iota(jnp.int32, (ROWS, ROWS), 1)
    low = jnp.where(core == 0, cross[...], swapped[...])
    high = jnp.where(core == 0, swapped[...], cross[...])
    acc = -emitted(mine[ROWS:], window[...])
    for i, block in enumerate((low, window[...], high)):
        count = jnp.where(row == lane, -4.0, 0.0) if i == 1 else jnp.zeros((ROWS, ROWS), F32)
        for j in range(4):
            count += jnp.where(local[j : j + 1] == row + i * ROWS, 1.0, 0.0)
        acc += lax.dot_general(
            count * conductance[...],
            block,
            (((0,), (0,)), ((), ())),
            precision=lax.Precision.HIGHEST,
            preferred_element_type=F32,
        )
    out[...] = acc


def last_kernel(mine, other, side, window, absorbed, heating):
    a = mine[:ROWS] + other[:ROWS]
    absorbed[...] = a
    heating[...] = a + side[...] - emitted(other[ROWS:], window[...])


def call(kernel, count, out_shape, scratch=(), in_specs=None, cost=None):
    single = not isinstance(out_shape, (list, tuple))
    return pl.pallas_call(
        kernel,
        out_shape=out_shape,
        in_specs=in_specs if in_specs is not None else vspec(count),
        out_specs=vspec(1)[0] if single else vspec(len(out_shape)),
        scratch_shapes=list(scratch),
        compiler_params=pltpu.CompilerParams(**PARAMS),
        cost_estimate=cost,
    )


def row_perm(move):
    return [
        ((z * NX + x) * 2 + c, (lambda a: (a[0] * NX + a[1]) * 2 + a[2])(move(z, x, c)))
        for z in range(NZ)
        for x in range(NX)
        for c in range(2)
    ]


CORE = row_perm(lambda z, x, c: (z, x, 1 - c))
XS = [row_perm(lambda z, x, c, d=d: (z, (x + d) % NX, c)) for d in range(NX)]
ZS = [row_perm(lambda z, x, c, d=d: ((z + d) % NZ, x, c)) for d in range(NZ)]
CROSS = [(i, (i + 1 if i % 2 else i - 1) % 32) for i in range(32)]
YS = [[(h * NY + y, h * NY + (y + d) % NY) for h in range(2) for y in range(NY)] for d in range(NY)]
HI = [(i, (i + NY) % (2 * NY)) for i in range(2 * NY)]


def body(gebhart, temps, emissivity, band_edges, conductance, neighbours):
    orbits, panels = temps.shape
    g = gebhart.reshape(NZ, NX, 2, ROWS, panels)
    half = NZ * ROWS
    hbm = pl.BlockSpec(memory_space=pltpu.HBM)
    bf = jnp.bfloat16
    dma = pltpu.SemaphoreType.DMA
    block = sds(ROWS, orbits)
    message = sds(ROWS + 8, orbits)
    rows = sds(2, NX, ROWS, panels, dtype=bf)
    pair = sds(2 * ROWS, orbits)
    cost = pl.CostEstimate(flops=PRODUCT_FLOPS, bytes_accessed=0, transcendentals=0)
    pause = pl.CostEstimate(flops=PAUSE_FLOPS, bytes_accessed=0, transcendentals=0)
    far = [
        pltpu.with_memory_space_constraint(a, pltpu.HBM)
        for a in (band_edges, emissivity, temps, g)
    ]
    u_a, p, g1, g2, g3, win, par = call(
        first_kernel,
        4,
        [sds(PART + ROWS, orbits), sds(orbits, panels, dtype=bf), *[rows] * 3, block, sds(8, orbits)],
        in_specs=[hbm] * 4,
        scratch=[
            VMEM((orbits, panels), F32),
            VMEM(rows.shape, bf),
            VMEM((1, panels), F32),
            pltpu.SMEM((1, 2), jnp.int32),
            dma((4,)),
            dma((4, 2)),
            dma((2,)),
        ],
        cost=cost,
    )(*far)
    u_a = lax.ppermute(u_a, "row", CORE)
    t_a = call(product_kernel, 2, sds(PART, orbits), cost=cost)(p, g2)
    u_b = call(product_kernel, 3, sds(PART, orbits), cost=cost)(p, g1, t_a)
    u_b = lax.ppermute(u_b, "row", CORE)
    *s_a, swapped = call(add_kernel, 2, [pair] * NX + [block])(t_a, u_a)
    x_a = [lax.ppermute(s_a[d], "row", XS[d]) for d in (2, 1, 3)]
    s_b = call(product_add_kernel, 4, [pair] * NX, scratch=[VMEM((PART, orbits), F32)], cost=cost)(
        p, g3, u_b, s_a[0]
    )
    x_b = [lax.ppermute(s_b[d], "row", XS[d]) for d in (2, 1, 3)]
    z2, z1, win = call(x_sum_carry_kernel, 5, [block] * 3)(s_a[0], *x_a, win)
    z2 = lax.ppermute(z2, "row", ZS[2])
    z1 = lax.ppermute(z1, "row", ZS[1])
    cross = lax.ppermute(win, "row", CROSS)
    z3, z0 = call(x_sum_kernel, 4, [block] * 2, cost=pause)(s_b[0], *x_b)
    z3 = lax.ppermute(z3, "row", ZS[3])
    zsum = call(z_sum_kernel, 6, message)(z0, z1, z2, z3, par, cross)
    y_in = [lax.ppermute(zsum, "band", YS[d]) for d in (1, 2, 3)]
    mine = call(y_sum_kernel, 4, message)(zsum, *y_in)
    other = lax.ppermute(mine, "band", HI)
    side = call(side_kernel, 6, block)(
        neighbours.T, conductance.reshape(1, ROWS), swapped, win, cross, mine
    )
    absorbed, heating = call(last_kernel, 4, [block] * 2)(mine, other, side, win)
    return absorbed.T, heating.T


def solution(mesh):
    return jax.shard_map(
        body,
        mesh=mesh,
        in_specs=(
            P("band", None, "row"),
            P(None, "row"),
            P("band", "row"),
            P("band", None),
            P("row"),
            P("row", None),
        ),
        out_specs=(P(None, "row"), P(None, "row")),
        check_vma=False,
    )
```

```python
import math

import jax
import jax.numpy as jnp
from jax import lax
from jax.experimental import pallas as pl
from jax.experimental.pallas import tpu as pltpu
from jax.sharding import PartitionSpec as P

ROWS = 64
NX, NZ, NY = 4, 4, 4
F32 = jnp.float32
VMEM = pltpu.VMEM
PART = 2 * NX * ROWS
FIRST, SECOND = (2, 1), (3, 0)
PRODUCT_FLOPS = 2 * PART * 2048 * 16
POWER_SCALE = 6.0 * 15.0 / math.pi**4 / 300.0**4
LOG2E = 1.0 / math.log(2.0)
PARAMS = dict(vmem_limit_bytes=24 * 2**20)


def vspec(count):
    return [pl.BlockSpec(memory_space=VMEM)] * count


def sds(*shape, dtype=F32):
    return jax.ShapeDtypeStruct(shape, dtype)


def place():
    row = lax.axis_index("row")
    return row // (2 * NX), (row // 2) % NX, row % 2


def edge_terms(a):
    return a * -LOG2E, a, a * a * 0.5, a * a * a * (1.0 / 6.0)


def power_chunk(t, emis, lo, hi):
    r = pl.reciprocal(t, approx=True)
    r = r * (2.0 - t * r)
    parts = [
        jnp.exp2(scale * r) * (((a + t) * t + half_square) * t + sixth_cube)
        for scale, a, half_square, sixth_cube in (lo, hi)
    ]
    return (parts[1] - parts[0]) * (t * emis)


def dot_nt(a, b):
    return lax.dot_general(a, b, (((1,), (1,)), ((), ())), preferred_element_type=F32)


def fetch_rows(g_hbm, buf, sems, z, core, offsets):
    return [
        pltpu.make_async_copy(g_hbm.at[(z + d) % NZ, :, core], buf.at[i], sems.at[i])
        for i, d in enumerate(offsets)
    ]


def flat(g):
    return g[...].reshape(g.shape[0] * NX * ROWS, g.shape[3])


def first_kernel(
    edges_hbm, emis_hbm, t_hbm, g_hbm, u, p, g1, g2, g3, win, par, tbuf, gbuf, scaled, edges, tsem, gsem, ssem
):
    z, x, core = place()
    part = tbuf.shape[0] // 4
    small = [
        pltpu.make_async_copy(edges_hbm, edges, ssem.at[0]),
        pltpu.make_async_copy(emis_hbm, scaled, ssem.at[1]),
    ]
    tcopies = [
        pltpu.make_async_copy(
            t_hbm.at[pl.ds(i * part, part)], tbuf.at[pl.ds(i * part, part)], tsem.at[i]
        )
        for i in range(4)
    ]
    gcopies = [
        fetch_rows(g_hbm, gbuf, gsem.at[0], z, 1 - core, FIRST),
        fetch_rows(g_hbm, g1, gsem.at[1], z, 1 - core, SECOND),
        fetch_rows(g_hbm, g2, gsem.at[2], z, core, FIRST),
        fetch_rows(g_hbm, g3, gsem.at[3], z, core, SECOND),
    ]
    for c in small + tcopies:
        c.start()
    for c in small:
        c.wait()
    a_lo = 14388000.0 / jnp.full((1, 512), edges[0, 0].astype(F32))
    a_hi = 14388000.0 / jnp.full((1, 512), edges[0, 1].astype(F32))
    scaled[...] = scaled[...] * POWER_SCALE
    lane = lax.broadcasted_iota(jnp.int32, (8, 256), 1)
    line = jnp.broadcast_to(scaled[:, :256], (8, 256))
    line = jnp.where(lane == ROWS, a_lo[:, :256], line)
    par[...] = jnp.where(lane == ROWS + 1, a_hi[:, :256], line)
    lo, hi = edge_terms(a_lo), edge_terms(a_hi)
    for i in range(4):
        tcopies[i].wait()
        if i == 0:
            for c in gcopies[0] + gcopies[1] + gcopies[2] + gcopies[3]:
                c.start()

        @pl.loop(0, part // 16)
        def _(j):
            rows = pl.ds(i * part + j * 16, 16)
            for c in range(4):
                cols = pl.ds(c * 512, 512)
                p[rows, cols] = power_chunk(tbuf[rows, cols], scaled[:, cols], lo, hi).astype(
                    jnp.bfloat16
                )

    w = tbuf[:, :128].T[:ROWS]
    win[...] = w
    u[PART:] = w
    for c in gcopies[0]:
        c.wait()
    u[:PART] = dot_nt(flat(gbuf), p[...])
    for c in gcopies[1] + gcopies[2] + gcopies[3]:
        c.wait()


def product_kernel(p, g, *refs):
    t = refs[-1]
    t[...] = dot_nt(flat(g), p[...])


def spread(value, outs):
    z, x, core = place()
    for d in range(NX):
        for i in range(2):
            rows = pl.ds(pl.multiple_of((i * NX + (x + d) % NX) * ROWS, ROWS), ROWS)
            outs[d][i * ROWS : (i + 1) * ROWS] = value(rows)


def add_kernel(t, u, *outs):
    spread(lambda rows: t[rows] + u[rows], outs)
    outs[NX][...] = u[PART:]


def product_add_kernel(p, g, u, s, *refs):
    outs, t = refs[:-1], refs[-1]
    t[...] = dot_nt(flat(g), p[...])
    spread(lambda rows: t[rows] + u[rows], outs)


def x_sum_carry_kernel(a, b, c, d, cross, *outs):
    x_sum_kernel(a, b, c, d, *outs)


def x_sum_kernel(a, b, c, d, *outs):
    for i in range(2):
        rows = pl.ds(i * ROWS, ROWS)
        outs[i][...] = (a[rows] + b[rows]) + (c[rows] + d[rows])


def z_sum_kernel(a, b, c, d, par, out):
    out[:ROWS] = (a[...] + b[...]) + (c[...] + d[...])
    out[ROWS:] = par[...]


def y_sum_kernel(a, b, c, d, out):
    out[:ROWS] = (a[:ROWS] + b[:ROWS]) + (c[:ROWS] + d[:ROWS])
    for i, ref in enumerate((a, b, c, d)):
        out[ROWS + i : ROWS + i + 1] = ref[ROWS : ROWS + 1]
    out[ROWS + NY :] = jnp.zeros((8 - NY, out.shape[1]), F32)


def emitted(par, win):
    total = jnp.zeros(win.shape, F32)
    columns = jnp.broadcast_to(par, (8, par.shape[1]))[:, :128].T
    for i in range(NY):
        part = power_chunk(
            win,
            columns[:ROWS, i : i + 1],
            edge_terms(par[i, ROWS]),
            edge_terms(par[i, ROWS + 1]),
        )
        total += part.astype(jnp.bfloat16).astype(F32)
    return total


def side_kernel(neighbours, conductance, swapped, window, cross, mine, out):
    z, x, core = place()
    me = (z * NX + x) * 2 + core
    total = 32 * ROWS
    local = neighbours[...] - (me * ROWS - ROWS)
    local = jnp.where(local < 0, local + total, local)
    local = jnp.where(local >= total, local - total, local)
    row = lax.broadcasted_iota(jnp.int32, (ROWS, ROWS), 0)
    lane = lax.broadcasted_iota(jnp.int32, (ROWS, ROWS), 1)
    low = jnp.where(core == 0, cross[...], swapped[...])
    high = jnp.where(core == 0, swapped[...], cross[...])
    acc = -emitted(mine[ROWS:], window[...])
    for i, block in enumerate((low, window[...], high)):
        count = jnp.where(row == lane, -4.0, 0.0) if i == 1 else jnp.zeros((ROWS, ROWS), F32)
        for j in range(4):
            count += jnp.where(local[j : j + 1] == row + i * ROWS, 1.0, 0.0)
        acc += lax.dot_general(
            count * conductance[...],
            block,
            (((0,), (0,)), ((), ())),
            precision=lax.Precision.HIGHEST,
            preferred_element_type=F32,
        )
    out[...] = acc


def last_kernel(mine, other, side, window, absorbed, heating):
    a = mine[:ROWS] + other[:ROWS]
    absorbed[...] = a
    heating[...] = a + side[...] - emitted(other[ROWS:], window[...])


def call(kernel, count, out_shape, scratch=(), in_specs=None, cost=None):
    single = not isinstance(out_shape, (list, tuple))
    return pl.pallas_call(
        kernel,
        out_shape=out_shape,
        in_specs=in_specs if in_specs is not None else vspec(count),
        out_specs=vspec(1)[0] if single else vspec(len(out_shape)),
        scratch_shapes=list(scratch),
        compiler_params=pltpu.CompilerParams(**PARAMS),
        cost_estimate=cost,
    )


def row_perm(move):
    return [
        ((z * NX + x) * 2 + c, (lambda a: (a[0] * NX + a[1]) * 2 + a[2])(move(z, x, c)))
        for z in range(NZ)
        for x in range(NX)
        for c in range(2)
    ]


CORE = row_perm(lambda z, x, c: (z, x, 1 - c))
XS = [row_perm(lambda z, x, c, d=d: (z, (x + d) % NX, c)) for d in range(NX)]
ZS = [row_perm(lambda z, x, c, d=d: ((z + d) % NZ, x, c)) for d in range(NZ)]
CROSS = [
    (band * 32 + i, (band + 4 * ((i + step) // 32 != 0)) % 8 * 32 + (i + step) % 32)
    for band in range(8)
    for i in range(32)
    for step in [1 if i % 2 else -1]
]
YS = [[(h * NY + y, h * NY + (y + d) % NY) for h in range(2) for y in range(NY)] for d in range(NY)]
HI = [(i, (i + NY) % (2 * NY)) for i in range(2 * NY)]


def body(gebhart, temps, emissivity, band_edges, conductance, neighbours):
    orbits, panels = temps.shape
    g = gebhart.reshape(NZ, NX, 2, ROWS, panels)
    half = NZ * ROWS
    hbm = pl.BlockSpec(memory_space=pltpu.HBM)
    bf = jnp.bfloat16
    dma = pltpu.SemaphoreType.DMA
    block = sds(ROWS, orbits)
    message = sds(ROWS + 8, orbits)
    rows = sds(2, NX, ROWS, panels, dtype=bf)
    pair = sds(2 * ROWS, orbits)
    cost = pl.CostEstimate(flops=PRODUCT_FLOPS, bytes_accessed=0, transcendentals=0)
    far = [
        pltpu.with_memory_space_constraint(a, pltpu.HBM)
        for a in (band_edges, emissivity, temps, g)
    ]
    u_a, p, g1, g2, g3, win, par = call(
        first_kernel,
        4,
        [sds(PART + ROWS, orbits), sds(orbits, panels, dtype=bf), *[rows] * 3, block, sds(8, orbits)],
        in_specs=[hbm] * 4,
        scratch=[
            VMEM((orbits, panels), F32),
            VMEM(rows.shape, bf),
            VMEM((1, panels), F32),
            pltpu.SMEM((1, 2), jnp.int32),
            dma((4,)),
            dma((4, 2)),
            dma((2,)),
        ],
        cost=cost,
    )(*far)
    u_a = lax.ppermute(u_a, "row", CORE)
    t_a = call(product_kernel, 2, sds(PART, orbits), cost=cost)(p, g2)
    u_b = call(product_kernel, 3, sds(PART, orbits), cost=cost)(p, g1, t_a)
    u_b = lax.ppermute(u_b, "row", CORE)
    *s_a, swapped = call(add_kernel, 2, [pair] * NX + [block])(t_a, u_a)
    x_a = [lax.ppermute(s_a[d], "row", XS[d]) for d in (2, 1, 3)]
    cross = lax.ppermute(win, ("band", "row"), CROSS)
    s_b = call(product_add_kernel, 4, [pair] * NX, scratch=[VMEM((PART, orbits), F32)], cost=cost)(
        p, g3, u_b, s_a[0]
    )
    x_b = [lax.ppermute(s_b[d], "row", XS[d]) for d in (2, 1, 3)]
    z2, z1 = call(x_sum_carry_kernel, 5, [block] * 2)(s_a[0], *x_a, cross)
    z2 = lax.ppermute(z2, "row", ZS[2])
    z1 = lax.ppermute(z1, "row", ZS[1])
    z3, z0 = call(x_sum_kernel, 4, [block] * 2)(s_b[0], *x_b)
    z3 = lax.ppermute(z3, "row", ZS[3])
    zsum = call(z_sum_kernel, 5, message)(z0, z1, z2, z3, par)
    y_in = [lax.ppermute(zsum, "band", YS[d]) for d in (1, 2, 3)]
    mine = call(y_sum_kernel, 4, message)(zsum, *y_in)
    other = lax.ppermute(mine, "band", HI)
    side = call(side_kernel, 6, block)(
        neighbours.T, conductance.reshape(1, ROWS), swapped, win, cross, mine
    )
    absorbed, heating = call(last_kernel, 4, [block] * 2)(mine, other, side, win)
    return absorbed.T, heating.T


def solution(mesh):
    return jax.shard_map(
        body,
        mesh=mesh,
        in_specs=(
            P("band", None, "row"),
            P(None, "row"),
            P("band", "row"),
            P("band", None),
            P("row"),
            P("row", None),
        ),
        out_specs=(P(None, "row"), P(None, "row")),
        check_vma=False,
    )
```

```python
import math

import jax
import jax.numpy as jnp
from jax import lax
from jax.experimental import pallas as pl
from jax.experimental.pallas import tpu as pltpu
from jax.sharding import PartitionSpec as P

ROWS = 64
NX, NZ, NY = 4, 4, 4
F32 = jnp.float32
VMEM = pltpu.VMEM
PART = 2 * NX * ROWS
FIRST, SECOND = (2, 1), (3, 0)
PRODUCT_FLOPS = 2 * PART * 2048 * 16
POWER_SCALE = 6.0 * 15.0 / math.pi**4 / 300.0**4
LOG2E = 1.0 / math.log(2.0)
PARAMS = dict(vmem_limit_bytes=24 * 2**20)


def vspec(count):
    return [pl.BlockSpec(memory_space=VMEM)] * count


def sds(*shape, dtype=F32):
    return jax.ShapeDtypeStruct(shape, dtype)


def place():
    row = lax.axis_index("row")
    return row // (2 * NX), (row // 2) % NX, row % 2


def edge_terms(a):
    return a * -LOG2E, a, a * a * 0.5, a * a * a * (1.0 / 6.0)


def power_chunk(t, emis, lo, hi):
    r = pl.reciprocal(t, approx=True)
    r = r * (2.0 - t * r)
    parts = [
        jnp.exp2(scale * r) * (((a + t) * t + half_square) * t + sixth_cube)
        for scale, a, half_square, sixth_cube in (lo, hi)
    ]
    return (parts[1] - parts[0]) * (t * emis)


def dot_nt(a, b):
    return lax.dot_general(a, b, (((1,), (1,)), ((), ())), preferred_element_type=F32)


def fetch_rows(g_hbm, buf, sems, z, core, offsets):
    return [
        pltpu.make_async_copy(g_hbm.at[(z + d) % NZ, :, core], buf.at[i], sems.at[i])
        for i, d in enumerate(offsets)
    ]


def flat(g):
    return g[...].reshape(g.shape[0] * NX * ROWS, g.shape[3])


def first_kernel(
    edges_hbm, emis_hbm, t_hbm, g_hbm, u, p, g1, g2, g3, win, par, tbuf, gbuf, scaled, edges, tsem, gsem, ssem
):
    z, x, core = place()
    part = tbuf.shape[0] // 4
    small = [
        pltpu.make_async_copy(edges_hbm, edges, ssem.at[0]),
        pltpu.make_async_copy(emis_hbm, scaled, ssem.at[1]),
    ]
    tcopies = [
        pltpu.make_async_copy(
            t_hbm.at[pl.ds(i * part, part)], tbuf.at[pl.ds(i * part, part)], tsem.at[i]
        )
        for i in range(4)
    ]
    gcopies = [
        fetch_rows(g_hbm, gbuf, gsem.at[0], z, 1 - core, FIRST),
        fetch_rows(g_hbm, g1, gsem.at[1], z, 1 - core, SECOND),
        fetch_rows(g_hbm, g2, gsem.at[2], z, core, FIRST),
        fetch_rows(g_hbm, g3, gsem.at[3], z, core, SECOND),
    ]
    for c in small + tcopies:
        c.start(priority=0)
    for c in gcopies[0] + gcopies[2] + gcopies[1] + gcopies[3]:
        c.start(priority=1)
    for c in small:
        c.wait()
    a_lo = 14388000.0 / jnp.full((1, 512), edges[0, 0].astype(F32))
    a_hi = 14388000.0 / jnp.full((1, 512), edges[0, 1].astype(F32))
    scaled[...] = scaled[...] * POWER_SCALE
    lane = lax.broadcasted_iota(jnp.int32, (8, 256), 1)
    line = jnp.broadcast_to(scaled[:, :256], (8, 256))
    line = jnp.where(lane == ROWS, a_lo[:, :256], line)
    par[...] = jnp.where(lane == ROWS + 1, a_hi[:, :256], line)
    lo, hi = edge_terms(a_lo), edge_terms(a_hi)
    for i in range(4):
        tcopies[i].wait()

        @pl.loop(0, part // 16)
        def _(j):
            rows = pl.ds(i * part + j * 16, 16)
            for c in range(4):
                cols = pl.ds(c * 512, 512)
                p[rows, cols] = power_chunk(tbuf[rows, cols], scaled[:, cols], lo, hi).astype(
                    jnp.bfloat16
                )

    w = tbuf[:, :128].T[:ROWS]
    win[...] = w
    u[PART:] = w
    for c in gcopies[0]:
        c.wait()
    u[:PART] = dot_nt(flat(gbuf), p[...])
    for c in gcopies[1] + gcopies[2] + gcopies[3]:
        c.wait()


def product_kernel(p, g, *refs):
    t = refs[-1]
    t[...] = dot_nt(flat(g), p[...])


def spread(value, outs):
    z, x, core = place()
    for d in range(NX):
        for i in range(2):
            rows = pl.ds(pl.multiple_of((i * NX + (x + d) % NX) * ROWS, ROWS), ROWS)
            outs[d][i * ROWS : (i + 1) * ROWS] = value(rows)


def add_kernel(t, u, *outs):
    spread(lambda rows: t[rows] + u[rows], outs)
    outs[NX][...] = u[PART:]


def product_add_kernel(p, g, u, s, *refs):
    outs, t = refs[:-1], refs[-1]
    t[...] = dot_nt(flat(g), p[...])
    spread(lambda rows: t[rows] + u[rows], outs)


def x_sum_carry_kernel(a, b, c, d, cross, *outs):
    x_sum_kernel(a, b, c, d, *outs)


def x_sum_kernel(a, b, c, d, *outs):
    for i in range(2):
        rows = pl.ds(i * ROWS, ROWS)
        outs[i][...] = (a[rows] + b[rows]) + (c[rows] + d[rows])


def z_sum_kernel(a, b, c, d, par, out):
    out[:ROWS] = (a[...] + b[...]) + (c[...] + d[...])
    out[ROWS:] = par[...]


def y_sum_kernel(a, b, c, d, out):
    out[:ROWS] = (a[:ROWS] + b[:ROWS]) + (c[:ROWS] + d[:ROWS])
    for i, ref in enumerate((a, b, c, d)):
        out[ROWS + i : ROWS + i + 1] = ref[ROWS : ROWS + 1]
    out[ROWS + NY :] = jnp.zeros((8 - NY, out.shape[1]), F32)


def emitted(par, win):
    total = jnp.zeros(win.shape, F32)
    columns = jnp.broadcast_to(par, (8, par.shape[1]))[:, :128].T
    for i in range(NY):
        part = power_chunk(
            win,
            columns[:ROWS, i : i + 1],
            edge_terms(par[i, ROWS]),
            edge_terms(par[i, ROWS + 1]),
        )
        total += part.astype(jnp.bfloat16).astype(F32)
    return total


def side_kernel(neighbours, conductance, swapped, window, cross, mine, out):
    z, x, core = place()
    me = (z * NX + x) * 2 + core
    total = 32 * ROWS
    local = neighbours[...] - (me * ROWS - ROWS)
    local = jnp.where(local < 0, local + total, local)
    local = jnp.where(local >= total, local - total, local)
    row = lax.broadcasted_iota(jnp.int32, (ROWS, ROWS), 0)
    lane = lax.broadcasted_iota(jnp.int32, (ROWS, ROWS), 1)
    low = jnp.where(core == 0, cross[...], swapped[...])
    high = jnp.where(core == 0, swapped[...], cross[...])
    acc = -emitted(mine[ROWS:], window[...])
    for i, block in enumerate((low, window[...], high)):
        count = jnp.where(row == lane, -4.0, 0.0) if i == 1 else jnp.zeros((ROWS, ROWS), F32)
        for j in range(4):
            count += jnp.where(local[j : j + 1] == row + i * ROWS, 1.0, 0.0)
        acc += lax.dot_general(
            count * conductance[...],
            block,
            (((0,), (0,)), ((), ())),
            precision=lax.Precision.HIGHEST,
            preferred_element_type=F32,
        )
    out[...] = acc


def last_kernel(mine, other, side, window, absorbed, heating):
    a = mine[:ROWS] + other[:ROWS]
    absorbed[...] = a
    heating[...] = a + side[...] - emitted(other[ROWS:], window[...])


def call(kernel, count, out_shape, scratch=(), in_specs=None, cost=None):
    single = not isinstance(out_shape, (list, tuple))
    return pl.pallas_call(
        kernel,
        out_shape=out_shape,
        in_specs=in_specs if in_specs is not None else vspec(count),
        out_specs=vspec(1)[0] if single else vspec(len(out_shape)),
        scratch_shapes=list(scratch),
        compiler_params=pltpu.CompilerParams(**PARAMS),
        cost_estimate=cost,
    )


def row_perm(move):
    return [
        ((z * NX + x) * 2 + c, (lambda a: (a[0] * NX + a[1]) * 2 + a[2])(move(z, x, c)))
        for z in range(NZ)
        for x in range(NX)
        for c in range(2)
    ]


CORE = row_perm(lambda z, x, c: (z, x, 1 - c))
XS = [row_perm(lambda z, x, c, d=d: (z, (x + d) % NX, c)) for d in range(NX)]
ZS = [row_perm(lambda z, x, c, d=d: ((z + d) % NZ, x, c)) for d in range(NZ)]
CROSS = [
    (band * 32 + i, (band + 4 * ((i + step) // 32 != 0)) % 8 * 32 + (i + step) % 32)
    for band in range(8)
    for i in range(32)
    for step in [1 if i % 2 else -1]
]
YS = [[(h * NY + y, h * NY + (y + d) % NY) for h in range(2) for y in range(NY)] for d in range(NY)]
HI = [(i, (i + NY) % (2 * NY)) for i in range(2 * NY)]


def body(gebhart, temps, emissivity, band_edges, conductance, neighbours):
    orbits, panels = temps.shape
    g = gebhart.reshape(NZ, NX, 2, ROWS, panels)
    half = NZ * ROWS
    hbm = pl.BlockSpec(memory_space=pltpu.HBM)
    bf = jnp.bfloat16
    dma = pltpu.SemaphoreType.DMA
    block = sds(ROWS, orbits)
    message = sds(ROWS + 8, orbits)
    rows = sds(2, NX, ROWS, panels, dtype=bf)
    pair = sds(2 * ROWS, orbits)
    cost = pl.CostEstimate(flops=PRODUCT_FLOPS, bytes_accessed=0, transcendentals=0)
    far = [
        pltpu.with_memory_space_constraint(a, pltpu.HBM)
        for a in (band_edges, emissivity, temps, g)
    ]
    u_a, p, g1, g2, g3, win, par = call(
        first_kernel,
        4,
        [sds(PART + ROWS, orbits), sds(orbits, panels, dtype=bf), *[rows] * 3, block, sds(8, orbits)],
        in_specs=[hbm] * 4,
        scratch=[
            VMEM((orbits, panels), F32),
            VMEM(rows.shape, bf),
            VMEM((1, panels), F32),
            pltpu.SMEM((1, 2), jnp.int32),
            dma((4,)),
            dma((4, 2)),
            dma((2,)),
        ],
        cost=cost,
    )(*far)
    u_a = lax.ppermute(u_a, "row", CORE)
    t_a = call(product_kernel, 2, sds(PART, orbits), cost=cost)(p, g2)
    u_b = call(product_kernel, 3, sds(PART, orbits), cost=cost)(p, g1, t_a)
    u_b = lax.ppermute(u_b, "row", CORE)
    *s_a, swapped = call(add_kernel, 2, [pair] * NX + [block])(t_a, u_a)
    x_a = [lax.ppermute(s_a[d], "row", XS[d]) for d in (2, 1, 3)]
    cross = lax.ppermute(win, ("band", "row"), CROSS)
    s_b = call(product_add_kernel, 4, [pair] * NX, scratch=[VMEM((PART, orbits), F32)], cost=cost)(
        p, g3, u_b, s_a[0]
    )
    x_b = [lax.ppermute(s_b[d], "row", XS[d]) for d in (2, 1, 3)]
    z2, z1 = call(x_sum_carry_kernel, 5, [block] * 2)(s_a[0], *x_a, cross)
    z2 = lax.ppermute(z2, "row", ZS[2])
    z1 = lax.ppermute(z1, "row", ZS[1])
    z3, z0 = call(x_sum_kernel, 4, [block] * 2)(s_b[0], *x_b)
    z3 = lax.ppermute(z3, "row", ZS[3])
    zsum = call(z_sum_kernel, 5, message)(z0, z1, z2, z3, par)
    y_in = [lax.ppermute(zsum, "band", YS[d]) for d in (1, 2, 3)]
    mine = call(y_sum_kernel, 4, message)(zsum, *y_in)
    other = lax.ppermute(mine, "band", HI)
    side = call(side_kernel, 6, block)(
        neighbours.T, conductance.reshape(1, ROWS), swapped, win, cross, mine
    )
    absorbed, heating = call(last_kernel, 4, [block] * 2)(mine, other, side, win)
    return absorbed.T, heating.T


def solution(mesh):
    return jax.shard_map(
        body,
        mesh=mesh,
        in_specs=(
            P("band", None, "row"),
            P(None, "row"),
            P("band", "row"),
            P("band", None),
            P("row"),
            P("row", None),
        ),
        out_specs=(P(None, "row"), P(None, "row")),
        check_vma=False,
    )
```

```python
import math

import jax
import jax.numpy as jnp
from jax import lax
from jax.experimental import pallas as pl
from jax.experimental.pallas import tpu as pltpu
from jax.sharding import PartitionSpec as P

ROWS = 64
NX, NZ, NY = 4, 4, 4
F32 = jnp.float32
VMEM = pltpu.VMEM
PART = 2 * NX * ROWS
PRODUCT_FLOPS = 2 * PART * 2048 * 16
POWER_SCALE = 6.0 * 15.0 / math.pi**4 / 300.0**4
LOG2E = 1.0 / math.log(2.0)
PARAMS = dict(vmem_limit_bytes=24 * 2**20)


def vspec(count):
    return [pl.BlockSpec(memory_space=VMEM)] * count


def sds(*shape, dtype=F32):
    return jax.ShapeDtypeStruct(shape, dtype)


def place():
    row = lax.axis_index("row")
    return row // (2 * NX), (row // 2) % NX, row % 2


def ahead(core):
    return 1 + 2 * core


def z_offsets(core):
    return (2, ahead(core)), (4 - ahead(core), 0)


def edge_terms(a):
    return a * -LOG2E, a, a * a * 0.5, a * a * a * (1.0 / 6.0)


def power_chunk(t, emis, lo, hi):
    r = pl.reciprocal(t, approx=True)
    r = r * (2.0 - t * r)
    parts = [
        jnp.exp2(scale * r) * (((a + t) * t + half_square) * t + sixth_cube)
        for scale, a, half_square, sixth_cube in (lo, hi)
    ]
    return (parts[1] - parts[0]) * (t * emis)


def dot_nt(a, b):
    return lax.dot_general(a, b, (((1,), (1,)), ((), ())), preferred_element_type=F32)


def fetch_rows(g_hbm, buf, sems, z, core, offsets):
    return [
        pltpu.make_async_copy(g_hbm.at[(z + d) % NZ, :, core], buf.at[i], sems.at[i])
        for i, d in enumerate(offsets)
    ]


def flat(g):
    return g[...].reshape(g.shape[0] * NX * ROWS, g.shape[3])


def first_kernel(
    edges_hbm, emis_hbm, t_hbm, g_hbm, u, p, g1, g2, g3, win, par, tbuf, gbuf, scaled, edges, tsem, gsem, ssem
):
    z, x, core = place()
    part = tbuf.shape[0] // 4
    small = [
        pltpu.make_async_copy(edges_hbm, edges, ssem.at[0]),
        pltpu.make_async_copy(emis_hbm, scaled, ssem.at[1]),
    ]
    tcopies = [
        pltpu.make_async_copy(
            t_hbm.at[pl.ds(i * part, part)], tbuf.at[pl.ds(i * part, part)], tsem.at[i]
        )
        for i in range(4)
    ]
    gcopies = [
        fetch_rows(g_hbm, gbuf, gsem.at[0], z, 1 - core, z_offsets(1 - core)[0]),
        fetch_rows(g_hbm, g1, gsem.at[1], z, 1 - core, z_offsets(1 - core)[1]),
        fetch_rows(g_hbm, g2, gsem.at[2], z, core, z_offsets(core)[0]),
        fetch_rows(g_hbm, g3, gsem.at[3], z, core, z_offsets(core)[1]),
    ]
    for c in small + tcopies:
        c.start()
    for c in gcopies[0] + gcopies[2] + gcopies[1] + gcopies[3]:
        c.start(priority=1)
    for c in small:
        c.wait()
    a_lo = 14388000.0 / jnp.full((1, 512), edges[0, 0].astype(F32))
    a_hi = 14388000.0 / jnp.full((1, 512), edges[0, 1].astype(F32))
    scaled[...] = scaled[...] * POWER_SCALE
    lane = lax.broadcasted_iota(jnp.int32, (8, 256), 1)
    line = jnp.broadcast_to(scaled[:, :256], (8, 256))
    line = jnp.where(lane == ROWS, a_lo[:, :256], line)
    par[...] = jnp.where(lane == ROWS + 1, a_hi[:, :256], line)
    lo, hi = edge_terms(a_lo), edge_terms(a_hi)
    for i in range(4):
        tcopies[i].wait()

        @pl.loop(0, part // 16)
        def _(j):
            rows = pl.ds(i * part + j * 16, 16)
            for c in range(4):
                cols = pl.ds(c * 512, 512)
                p[rows, cols] = power_chunk(tbuf[rows, cols], scaled[:, cols], lo, hi).astype(
                    jnp.bfloat16
                )

    w = tbuf[:, :128].T[:ROWS]
    win[...] = w
    u[PART:] = w
    for c in gcopies[0]:
        c.wait()
    u[:PART] = dot_nt(flat(gbuf), p[...])
    for c in gcopies[1] + gcopies[2] + gcopies[3]:
        c.wait()


def product_kernel(p, g, *refs):
    t = refs[-1]
    t[...] = dot_nt(flat(g), p[...])


def spread(value, outs):
    z, x, core = place()
    for out, d in zip(outs, (0, ahead(core), 2, 4 - ahead(core))):
        for i in range(2):
            rows = pl.ds(pl.multiple_of((i * NX + (x + d) % NX) * ROWS, ROWS), ROWS)
            out[i * ROWS : (i + 1) * ROWS] = value(rows)


def add_kernel(t, u, *outs):
    spread(lambda rows: t[rows] + u[rows], outs[:NX])
    outs[1][2 * ROWS :] = u[PART:]
    outs[NX][...] = u[PART:]


def product_add_kernel(p, g, u, s, *refs):
    outs, t = refs[:-1], refs[-1]
    t[...] = dot_nt(flat(g), p[...])
    spread(lambda rows: t[rows] + u[rows], outs)


def x_sum_kernel(a, b, c, d, *outs):
    for i in range(2):
        rows = pl.ds(i * ROWS, ROWS)
        outs[i][:ROWS] = (a[rows] + b[rows]) + (c[rows] + d[rows])


def x_sum_carry_kernel(a, b, c, d, *outs):
    x_sum_kernel(a, b, c, d, *outs)
    outs[1][ROWS:] = b[2 * ROWS :]


def x_sum_rest_kernel(a, b, c, d, after, *outs):
    x_sum_kernel(a, b, c, d, *outs)


def z_part_kernel(a, b, c, out):
    out[...] = (a[...] + b[:ROWS]) + c[...]


def z_sum_kernel(a, b, par, out):
    out[:ROWS] = a[...] + b[...]
    out[ROWS:] = par[...]


def y_sum_kernel(a, b, c, d, out):
    out[:ROWS] = (a[:ROWS] + b[:ROWS]) + (c[:ROWS] + d[:ROWS])
    for i, ref in enumerate((a, b, c, d)):
        out[ROWS + i : ROWS + i + 1] = ref[ROWS : ROWS + 1]
    out[ROWS + NY :] = jnp.zeros((8 - NY, out.shape[1]), F32)


def emitted(par, win):
    total = jnp.zeros(win.shape, F32)
    columns = jnp.broadcast_to(par, (8, par.shape[1]))[:, :128].T
    for i in range(NY):
        part = power_chunk(
            win,
            columns[:ROWS, i : i + 1],
            edge_terms(par[i, ROWS]),
            edge_terms(par[i, ROWS + 1]),
        )
        total += part.astype(jnp.bfloat16).astype(F32)
    return total


def side_kernel(neighbours, conductance, swapped, window, by_x, by_z, mine, out):
    z, x, core = place()
    me = (z * NX + x) * 2 + core
    total = 32 * ROWS
    local = neighbours[...] - (me * ROWS - ROWS)
    local = jnp.where(local < 0, local + total, local)
    local = jnp.where(local >= total, local - total, local)
    row = lax.broadcasted_iota(jnp.int32, (ROWS, ROWS), 0)
    lane = lax.broadcasted_iota(jnp.int32, (ROWS, ROWS), 1)
    cross = jnp.where(x == 3 * core, by_z[ROWS:], by_x[2 * ROWS :])
    low = jnp.where(core == 0, cross, swapped[...])
    high = jnp.where(core == 0, swapped[...], cross)
    acc = -emitted(mine[ROWS:], window[...])
    for i, block in enumerate((low, window[...], high)):
        count = jnp.where(row == lane, -4.0, 0.0) if i == 1 else jnp.zeros((ROWS, ROWS), F32)
        for j in range(4):
            count += jnp.where(local[j : j + 1] == row + i * ROWS, 1.0, 0.0)
        acc += lax.dot_general(
            count * conductance[...],
            block,
            (((0,), (0,)), ((), ())),
            precision=lax.Precision.HIGHEST,
            preferred_element_type=F32,
        )
    out[...] = acc


def last_kernel(mine, other, side, window, absorbed, heating):
    a = mine[:ROWS] + other[:ROWS]
    absorbed[...] = a
    heating[...] = a + side[...] - emitted(other[ROWS:], window[...])


def call(kernel, count, out_shape, scratch=(), in_specs=None, cost=None):
    single = not isinstance(out_shape, (list, tuple))
    return pl.pallas_call(
        kernel,
        out_shape=out_shape,
        in_specs=in_specs if in_specs is not None else vspec(count),
        out_specs=vspec(1)[0] if single else vspec(len(out_shape)),
        scratch_shapes=list(scratch),
        compiler_params=pltpu.CompilerParams(**PARAMS),
        cost_estimate=cost,
    )


def row_perm(move):
    return [
        ((z * NX + x) * 2 + c, (lambda a: (a[0] * NX + a[1]) * 2 + a[2])(move(z, x, c)))
        for z in range(NZ)
        for x in range(NX)
        for c in range(2)
    ]


CORE = row_perm(lambda z, x, c: (z, x, 1 - c))
X2 = row_perm(lambda z, x, c: (z, (x + 2) % NX, c))
XF = row_perm(lambda z, x, c: (z, (x + 1 + 2 * c) % NX, c))
XB = row_perm(lambda z, x, c: (z, (x + 3 - 2 * c) % NX, c))
Z2 = row_perm(lambda z, x, c: ((z + 2) % NZ, x, c))
ZF = row_perm(lambda z, x, c: ((z + 1 + 2 * c) % NZ, x, c))
ZB = row_perm(lambda z, x, c: ((z + 3 - 2 * c) % NZ, x, c))
YS = [[(h * NY + y, h * NY + (y + d) % NY) for h in range(2) for y in range(NY)] for d in range(NY)]
HI = [(i, (i + NY) % (2 * NY)) for i in range(2 * NY)]


def body(gebhart, temps, emissivity, band_edges, conductance, neighbours):
    orbits, panels = temps.shape
    g = gebhart.reshape(NZ, NX, 2, ROWS, panels)
    half = NZ * ROWS
    hbm = pl.BlockSpec(memory_space=pltpu.HBM)
    bf = jnp.bfloat16
    dma = pltpu.SemaphoreType.DMA
    block = sds(ROWS, orbits)
    message = sds(ROWS + 8, orbits)
    rows = sds(2, NX, ROWS, panels, dtype=bf)
    pair = sds(2 * ROWS, orbits)
    cost = pl.CostEstimate(flops=PRODUCT_FLOPS, bytes_accessed=0, transcendentals=0)
    far = [
        pltpu.with_memory_space_constraint(a, pltpu.HBM)
        for a in (band_edges, emissivity, temps, g)
    ]
    u_a, p, g1, g2, g3, win, par = call(
        first_kernel,
        4,
        [sds(PART + ROWS, orbits), sds(orbits, panels, dtype=bf), *[rows] * 3, block, sds(8, orbits)],
        in_specs=[hbm] * 4,
        scratch=[
            VMEM((orbits, panels), F32),
            VMEM(rows.shape, bf),
            VMEM((1, panels), F32),
            pltpu.SMEM((1, 2), jnp.int32),
            dma((4,)),
            dma((4, 2)),
            dma((2,)),
        ],
        cost=cost,
    )(*far)
    u_a = lax.ppermute(u_a, "row", CORE)
    t_a = call(product_kernel, 2, sds(PART, orbits), cost=cost)(p, g2)
    u_b = call(product_kernel, 3, sds(PART, orbits), cost=cost)(p, g1, t_a)
    u_b = lax.ppermute(u_b, "row", CORE)
    long = sds(3 * ROWS, orbits)
    *s_a, swapped = call(add_kernel, 2, [pair, long, pair, pair, block])(t_a, u_a)
    x_a = [lax.ppermute(s_a[i], "row", perm) for i, perm in ((2, X2), (1, XF), (3, XB))]
    s_b = call(product_add_kernel, 4, [pair] * NX, scratch=[VMEM((PART, orbits), F32)], cost=cost)(
        p, g3, u_b, s_a[0]
    )
    x_b = [lax.ppermute(s_b[i], "row", perm) for i, perm in ((2, X2), (1, XF), (3, XB))]
    z2, zf = call(x_sum_carry_kernel, 4, [block, pair])(s_a[0], x_a[1], x_a[0], x_a[2])
    z2_out = z2
    z2 = lax.ppermute(z2, "row", Z2)
    zf = lax.ppermute(zf, "row", ZF)
    zb, z0 = call(x_sum_rest_kernel, 5, [block] * 2)(s_b[0], x_b[1], x_b[0], x_b[2], z2_out)
    zb = lax.ppermute(zb, "row", ZB)
    zsum = call(z_part_kernel, 3, block)(z0, zf, z2)
    zsum = call(z_sum_kernel, 3, message)(zsum, zb, par)
    y_in = [lax.ppermute(zsum, "band", YS[d]) for d in (3, 1, 2)]

    mine = call(y_sum_kernel, 4, message)(zsum, *y_in)
    other = lax.ppermute(mine, "band", HI)
    side = call(side_kernel, 7, block)(
        neighbours.T, conductance.reshape(1, ROWS), swapped, win, x_a[1], zf, mine
    )
    absorbed, heating = call(last_kernel, 4, [block] * 2)(mine, other, side, win)
    return absorbed.T, heating.T


def solution(mesh):
    return jax.shard_map(
        body,
        mesh=mesh,
        in_specs=(
            P("band", None, "row"),
            P(None, "row"),
            P("band", "row"),
            P("band", None),
            P("row"),
            P("row", None),
        ),
        out_specs=(P(None, "row"), P(None, "row")),
        check_vma=False,
    )
```

```python
import math

import jax
import jax.numpy as jnp
from jax import lax
from jax.experimental import pallas as pl
from jax.experimental.pallas import tpu as pltpu
from jax.sharding import PartitionSpec as P

ROWS = 64
NX, NZ, NY = 4, 4, 4
F32 = jnp.float32
VMEM = pltpu.VMEM
PART = 2 * NX * ROWS
PRODUCT_FLOPS = 2 * PART * 2048 * 16
POWER_SCALE = 6.0 * 15.0 / math.pi**4 / 300.0**4
LOG2E = 1.0 / math.log(2.0)
PARAMS = dict(vmem_limit_bytes=24 * 2**20)


def vspec(count):
    return [pl.BlockSpec(memory_space=VMEM)] * count


def sds(*shape, dtype=F32):
    return jax.ShapeDtypeStruct(shape, dtype)


def place():
    row = lax.axis_index("row")
    return row // (2 * NX), (row // 2) % NX, row % 2


def ahead(core):
    return 1 + 2 * core


def z_offsets(core):
    return (2, ahead(core)), (4 - ahead(core), 0)


def edge_terms(a):
    return a * -LOG2E, a, a * a * 0.5, a * a * a * (1.0 / 6.0)


def power_chunk(t, emis, lo, hi):
    r = pl.reciprocal(t, approx=True)
    r = r * (2.0 - t * r)
    parts = [
        jnp.exp2(scale * r) * (((a + t) * t + half_square) * t + sixth_cube)
        for scale, a, half_square, sixth_cube in (lo, hi)
    ]
    return (parts[1] - parts[0]) * (t * emis)


def dot_nt(a, b):
    return lax.dot_general(a, b, (((1,), (1,)), ((), ())), preferred_element_type=F32)


def fetch_rows(g_hbm, buf, sems, z, core, offsets):
    return [
        pltpu.make_async_copy(g_hbm.at[(z + d) % NZ, :, core], buf.at[i], sems.at[i])
        for i, d in enumerate(offsets)
    ]


def flat(g):
    return g[...].reshape(g.shape[0] * NX * ROWS, g.shape[3])


def first_kernel(
    edges_hbm, emis_hbm, t_hbm, g_hbm, u, p, g1, g2, g3, win, par, tbuf, gbuf, scaled, edges, tsem, gsem, ssem
):
    z, x, core = place()
    part = tbuf.shape[0] // 4
    small = [
        pltpu.make_async_copy(edges_hbm, edges, ssem.at[0]),
        pltpu.make_async_copy(emis_hbm, scaled, ssem.at[1]),
    ]
    tcopies = [
        pltpu.make_async_copy(
            t_hbm.at[pl.ds(i * part, part)], tbuf.at[pl.ds(i * part, part)], tsem.at[i]
        )
        for i in range(4)
    ]
    gcopies = [
        fetch_rows(g_hbm, gbuf, gsem.at[0], z, 1 - core, z_offsets(1 - core)[0]),
        fetch_rows(g_hbm, g1, gsem.at[1], z, 1 - core, z_offsets(1 - core)[1]),
        fetch_rows(g_hbm, g2, gsem.at[2], z, core, z_offsets(core)[0]),
        fetch_rows(g_hbm, g3, gsem.at[3], z, core, z_offsets(core)[1]),
    ]
    for c in small + tcopies:
        c.start()
    for c in gcopies[0] + gcopies[2] + gcopies[1] + gcopies[3]:
        c.start(priority=1)
    for c in small:
        c.wait()
    a_lo = 14388000.0 / jnp.full((1, 512), edges[0, 0].astype(F32))
    a_hi = 14388000.0 / jnp.full((1, 512), edges[0, 1].astype(F32))
    scaled[...] = scaled[...] * POWER_SCALE
    lane = lax.broadcasted_iota(jnp.int32, (8, 256), 1)
    line = jnp.broadcast_to(scaled[:, :256], (8, 256))
    line = jnp.where(lane == ROWS, a_lo[:, :256], line)
    par[...] = jnp.where(lane == ROWS + 1, a_hi[:, :256], line)
    lo, hi = edge_terms(a_lo), edge_terms(a_hi)
    for i in range(4):
        tcopies[i].wait()

        @pl.loop(0, part // 16)
        def _(j):
            rows = pl.ds(i * part + j * 16, 16)
            for c in range(4):
                cols = pl.ds(c * 512, 512)
                p[rows, cols] = power_chunk(tbuf[rows, cols], scaled[:, cols], lo, hi).astype(
                    jnp.bfloat16
                )

    w = tbuf[:, :128].T[:ROWS]
    win[...] = w
    u[PART:] = w
    for c in gcopies[0]:
        c.wait()
    u[:PART] = dot_nt(flat(gbuf), p[...])
    for c in gcopies[1] + gcopies[2] + gcopies[3]:
        c.wait()


def product_kernel(p, g, *refs):
    t = refs[-1]
    t[...] = dot_nt(flat(g), p[...])


def spread(value, outs):
    z, x, core = place()
    for out, d in zip(outs, (0, ahead(core), 2, 4 - ahead(core))):
        for i in range(2):
            rows = pl.ds(pl.multiple_of((i * NX + (x + d) % NX) * ROWS, ROWS), ROWS)
            out[i * ROWS : (i + 1) * ROWS] = value(rows)


def add_kernel(t, u, *outs):
    spread(lambda rows: t[rows] + u[rows], outs[:NX])
    outs[1][2 * ROWS :] = u[PART:]
    outs[NX][...] = u[PART:]


def product_add_kernel(p, g, u, s, *refs):
    outs, t = refs[:-1], refs[-1]
    t[...] = dot_nt(flat(g), p[...])
    spread(lambda rows: t[rows] + u[rows], outs)


def x_sum_kernel(a, b, c, d, *outs):
    for i in range(2):
        rows = pl.ds(i * ROWS, ROWS)
        outs[i][:ROWS] = (a[rows] + b[rows]) + (c[rows] + d[rows])


def x_sum_carry_kernel(a, b, c, d, *outs):
    x_sum_kernel(a, b, c, d, *outs)
    outs[1][ROWS:] = b[2 * ROWS :]


def x_sum_rest_kernel(a, b, c, d, after, *outs):
    x_sum_kernel(a, b, c, d, *outs)


def z_part_kernel(a, b, c, out):
    out[...] = (a[...] + b[:ROWS]) + c[...]


def z_sum_kernel(a, b, par, out):
    out[:ROWS] = a[...] + b[...]
    out[ROWS:] = par[...]


def y_sum_kernel(a, b, c, d, out):
    out[:ROWS] = (a[:ROWS] + b[:ROWS]) + (c[:ROWS] + d[:ROWS])
    for i, ref in enumerate((a, b, c, d)):
        out[ROWS + i : ROWS + i + 1] = ref[ROWS : ROWS + 1]
    out[ROWS + NY :] = jnp.zeros((8 - NY, out.shape[1]), F32)


def emitted(par, win):
    total = jnp.zeros(win.shape, F32)
    columns = jnp.broadcast_to(par, (8, par.shape[1]))[:, :128].T
    for i in range(NY):
        part = power_chunk(
            win,
            columns[:ROWS, i : i + 1],
            edge_terms(par[i, ROWS]),
            edge_terms(par[i, ROWS + 1]),
        )
        total += part.astype(jnp.bfloat16).astype(F32)
    return total


def side_kernel(neighbours, conductance, swapped, window, by_x, by_z, mine, out):
    z, x, core = place()
    me = (z * NX + x) * 2 + core
    total = 32 * ROWS
    local = neighbours[...] - (me * ROWS - ROWS)
    local = jnp.where(local < 0, local + total, local)
    local = jnp.where(local >= total, local - total, local)
    row = lax.broadcasted_iota(jnp.int32, (ROWS, ROWS), 0)
    lane = lax.broadcasted_iota(jnp.int32, (ROWS, ROWS), 1)
    cross = jnp.where(x == 3 * core, by_z[ROWS:], by_x[2 * ROWS :])
    low = jnp.where(core == 0, cross, swapped[...])
    high = jnp.where(core == 0, swapped[...], cross)
    acc = -emitted(mine[ROWS:], window[...])
    for i, block in enumerate((low, window[...], high)):
        count = jnp.where(row == lane, -4.0, 0.0) if i == 1 else jnp.zeros((ROWS, ROWS), F32)
        for j in range(4):
            count += jnp.where(local[j : j + 1] == row + i * ROWS, 1.0, 0.0)
        acc += lax.dot_general(
            count * conductance[...],
            block,
            (((0,), (0,)), ((), ())),
            precision=lax.Precision.HIGHEST,
            preferred_element_type=F32,
        )
    out[...] = acc


def last_kernel(mine, other, side, window, absorbed, heating):
    a = mine[:ROWS] + other[:ROWS]
    absorbed[...] = a
    heating[...] = a + side[...] - emitted(other[ROWS:], window[...])


def call(kernel, count, out_shape, scratch=(), in_specs=None, cost=None):
    single = not isinstance(out_shape, (list, tuple))
    return pl.pallas_call(
        kernel,
        out_shape=out_shape,
        in_specs=in_specs if in_specs is not None else vspec(count),
        out_specs=vspec(1)[0] if single else vspec(len(out_shape)),
        scratch_shapes=list(scratch),
        compiler_params=pltpu.CompilerParams(**PARAMS),
        cost_estimate=cost,
    )


def row_perm(move):
    return [
        ((z * NX + x) * 2 + c, (lambda a: (a[0] * NX + a[1]) * 2 + a[2])(move(z, x, c)))
        for z in range(NZ)
        for x in range(NX)
        for c in range(2)
    ]


CORE = row_perm(lambda z, x, c: (z, x, 1 - c))
X2 = row_perm(lambda z, x, c: (z, (x + 2) % NX, c))
XF = row_perm(lambda z, x, c: (z, (x + 1 + 2 * c) % NX, c))
XB = row_perm(lambda z, x, c: (z, (x + 3 - 2 * c) % NX, c))
Z2 = row_perm(lambda z, x, c: ((z + 2) % NZ, x, c))
ZF = row_perm(lambda z, x, c: ((z + 1 + 2 * c) % NZ, x, c))
ZB = row_perm(lambda z, x, c: ((z + 3 - 2 * c) % NZ, x, c))
YS = [[(h * NY + y, h * NY + (y + d) % NY) for h in range(2) for y in range(NY)] for d in range(NY)]
HI = [(i, (i + NY) % (2 * NY)) for i in range(2 * NY)]


def body(gebhart, temps, emissivity, band_edges, conductance, neighbours):
    orbits, panels = temps.shape
    g = gebhart.reshape(NZ, NX, 2, ROWS, panels)
    half = NZ * ROWS
    hbm = pl.BlockSpec(memory_space=pltpu.HBM)
    bf = jnp.bfloat16
    dma = pltpu.SemaphoreType.DMA
    block = sds(ROWS, orbits)
    message = sds(ROWS + 8, orbits)
    rows = sds(2, NX, ROWS, panels, dtype=bf)
    pair = sds(2 * ROWS, orbits)
    cost = pl.CostEstimate(flops=PRODUCT_FLOPS, bytes_accessed=0, transcendentals=0)
    far = [
        pltpu.with_memory_space_constraint(a, pltpu.HBM)
        for a in (band_edges, emissivity, temps, g)
    ]
    u_a, p, g1, g2, g3, win, par = call(
        first_kernel,
        4,
        [sds(PART + ROWS, orbits), sds(orbits, panels, dtype=bf), *[rows] * 3, block, sds(8, orbits)],
        in_specs=[hbm] * 4,
        scratch=[
            VMEM((orbits, panels), F32),
            VMEM(rows.shape, bf),
            VMEM((1, panels), F32),
            pltpu.SMEM((1, 2), jnp.int32),
            dma((4,)),
            dma((4, 2)),
            dma((2,)),
        ],
        cost=cost,
    )(*far)
    u_a = lax.ppermute(u_a, "row", CORE)
    t_a = call(product_kernel, 2, sds(PART, orbits), cost=cost)(p, g2)
    u_b = call(product_kernel, 3, sds(PART, orbits), cost=cost)(p, g1, t_a)
    u_b = lax.ppermute(u_b, "row", CORE)
    long = sds(3 * ROWS, orbits)
    *s_a, swapped = call(add_kernel, 2, [pair, long, pair, pair, block])(t_a, u_a)
    x_a = [lax.ppermute(s_a[i], "row", perm) for i, perm in ((2, X2), (1, XF), (3, XB))]
    s_b = call(product_add_kernel, 4, [pair] * NX, scratch=[VMEM((PART, orbits), F32)], cost=cost)(
        p, g3, u_b, s_a[0]
    )
    x_b = [lax.ppermute(s_b[i], "row", perm) for i, perm in ((2, X2), (1, XF), (3, XB))]
    z2, zf = call(x_sum_carry_kernel, 4, [block, pair])(s_a[0], x_a[1], x_a[0], x_a[2])
    z2_out = z2
    z2 = lax.ppermute(z2, "row", Z2)
    zf = lax.ppermute(zf, "row", ZF)
    zb, z0 = call(x_sum_rest_kernel, 5, [block] * 2)(s_b[0], x_b[1], x_b[0], x_b[2], z2_out)
    zb = lax.ppermute(zb, "row", ZB)
    zsum = call(z_part_kernel, 3, block)(z0, zf, z2)
    zsum = call(z_sum_kernel, 3, message)(zsum, zb, par)
    y_in = [lax.ppermute(zsum, "band", YS[d]) for d in (3, 2, 1)]

    mine = call(y_sum_kernel, 4, message)(zsum, *y_in)
    other = lax.ppermute(mine, "band", HI)
    side = call(side_kernel, 7, block)(
        neighbours.T, conductance.reshape(1, ROWS), swapped, win, x_a[1], zf, mine
    )
    absorbed, heating = call(last_kernel, 4, [block] * 2)(mine, other, side, win)
    return absorbed.T, heating.T


def solution(mesh):
    return jax.shard_map(
        body,
        mesh=mesh,
        in_specs=(
            P("band", None, "row"),
            P(None, "row"),
            P("band", "row"),
            P("band", None),
            P("row"),
            P("row", None),
        ),
        out_specs=(P(None, "row"), P(None, "row")),
        check_vma=False,
    )
```
